512 devices in a mesh: dp: 16 (over z, core), shard: 32 (over x, y).
Axes of the slice: x: 4, y: 8, z: 8, core: 2. Of those that a mesh axis runs over, the one named last changes fastest.
Arguments:
- table: bfloat16 [32768, 160], P('shard'), may hold values from -6 to 6
- slot_rows: int32 [16, 32, 32, 32], P('dp', 'shard'), may hold values from 0 to 1023
- slot_counts: int32 [16, 32, 32], P('dp', 'shard'), may hold values from 8 to 32, as said below
- positions: int32 [8192, 128], P(('dp', 'shard')), may hold values from 0 to 1023
- fm_proj: bfloat16 [128, 8], replicated, may hold values from -0.5 to 0.5
- ln_gain: float32 [1024], replicated, may hold values from 0.1 to 1.9
- w_up: bfloat16 [1024, 4096], P(None, 'shard'), may hold values from -0.1875 to 0.1875
- w_down: bfloat16 [4096, 2560], P('shard'), may hold values from -0.09375 to 0.09375
- w_lcb: bfloat16 [112, 128], replicated, may hold values from -0.5 to 0.5
- cotangent: bfloat16 [8192, 128, 160], P(('dp', 'shard')), may hold values from -6 to 6
Outputs:
- mixed: bfloat16 [8192, 128, 160], P(('dp', 'shard'))
- grad_table: float32 [32768, 160], P('shard')
- grad_w_up: bfloat16 [1024, 4096], P('dp', 'shard')
- grad_w_down: bfloat16 [4096, 2560], P('shard', 'dp')
- grad_fm_proj: float32 [128, 8], replicated
- grad_w_lcb: float32 [112, 128], replicated
- grad_ln_gain: float32 [1024], replicated
The draws below stay inside these ranges and needn't reach their ends.
Inputs may be any that keep to these rules, and one draw needn't show every extreme that they name: `slot_counts`: every device has some owner to which all 32 of its slots are live.
All inputs are finite; a program needn't handle non-finite values.
Results may differ from the reference program's by a relative error of at most 0.018.
Values may be sent and summed in bfloat16 or wider, within the bound.
No kernel may reach another device: no remote copies, remote signals or barrier semaphores. Data moves between devices by JAX's collectives and lax.ppermute only.
A program may use at most 64 MiB of HBM per device.

```python
import jax
import jax.numpy as jnp
from jax import lax

D = 160
F = 128
K = 8
NF = 16
H = 4096
CAP = 32
B_DEV = 16
ROWS_DEV = 1024
SAMPLES = 8192
ROWS = 32768
N_DP = 16
N_SHARD = 32


def draw_slot_counts(key, part):
    key = jax.random.fold_in(key, 5)
    shape = (N_DP, N_SHARD, N_SHARD)
    divisor = jax.random.randint(key, shape, 1, 5)
    counts = CAP // divisor
    group = lax.broadcasted_iota(jnp.int32, shape, 0)
    member = lax.broadcasted_iota(jnp.int32, shape, 1)
    owner = lax.broadcasted_iota(jnp.int32, shape, 2)
    filled = owner == (member + 3 * group) % N_SHARD
    return jnp.where(filled, CAP, counts).astype(jnp.int32)


def set_ends(entries, key, least, high):
    longest = entries.shape.index(max(entries.shape))
    spots = []
    for shift in (0, 1):
        where = [jax.random.randint(jax.random.fold_in(key, axis), (), 0, length) for axis, length in enumerate(entries.shape)]
        where[longest] = (where[longest] + shift) % entries.shape[longest]
        spots.append(tuple(where))
    return entries.at[spots[0]].set(least).at[spots[1]].set(high)


def block_levels(key, dims, split, smallest, largest):
    factor_of, own = 1.0, jax.random.fold_in(key, 6)
    for dim, blocks in split:
        draws = jnp.exp(jax.random.uniform(jax.random.fold_in(own, dim), (blocks,), jnp.float32, smallest / len(split), largest / len(split)))
        factor_of = factor_of * jnp.repeat(draws, dims[dim] // blocks).reshape([-1 if axis == dim else 1 for axis in range(len(dims))])
    return factor_of


def gaussian(rng, dims, width, most, shards=(), kind=jnp.bfloat16):
    entries = width * jax.random.normal(rng, dims, jnp.float32)
    if shards:
        entries = entries * block_levels(rng, dims, shards, -0.22, 0.18)
    return jnp.clip(entries, -most, most).astype(kind)


def setup_inputs(seed: int = 0) -> dict:
    streams_of = jax.random.split(jax.random.key(seed), 11)
    table = gaussian(streams_of[0], (ROWS, D), 1.0, 6.0, ((0, 32),))
    slot_rows = set_ends(jax.random.randint(streams_of[1], (N_DP, N_SHARD, N_SHARD, CAP), 0, ROWS_DEV), jax.random.fold_in(streams_of[1], 1), 0, ROWS_DEV - 1).astype(jnp.int32)
    slot_counts = draw_slot_counts(jax.random.fold_in(streams_of[10], 71), 0)
    positions = set_ends(jax.random.randint(streams_of[3], (SAMPLES, F), 0, N_SHARD * CAP), jax.random.fold_in(streams_of[3], 1), 0, (N_SHARD * CAP) - 1).astype(jnp.int32)
    fm_proj = gaussian(streams_of[4], (F, K), F ** -0.5, 0.5)
    ln_gain = jnp.clip(1.0 + 0.18 * jax.random.normal(streams_of[5], (F * K,), jnp.float32), 0.1, 1.9)
    w_up = gaussian(streams_of[6], (F * K, H), (F * K) ** -0.5, 0.1875, ((1, 32),))
    w_down = gaussian(streams_of[7], (H, NF * D), H ** -0.5, 0.09375, ((0, 32),))
    w_lcb = gaussian(streams_of[8], (F - NF, F), F ** -0.5, 0.5)
    cotangent = gaussian(streams_of[9], (SAMPLES, F, D), 1.0, 6.0, ((0, 512),))
    return dict(table=table, slot_rows=slot_rows, slot_counts=slot_counts, positions=positions, fm_proj=fm_proj, ln_gain=ln_gain, w_up=w_up, w_down=w_down, w_lcb=w_lcb, cotangent=cotangent)


def rounded_sum(lefts, rights):

    def add_block(running, pair):
        term = jnp.dot(pair[0], pair[1], preferred_element_type=jnp.float32).astype(jnp.bfloat16)
        term = lax.optimization_barrier(term)
        return (running + term.astype(jnp.float32), None)
    initial = jnp.zeros((lefts.shape[1], rights.shape[2]), jnp.float32)
    total, unused = lax.scan(add_block, initial, (lefts, rights))
    return total

def layer_norm(flat):
    center = flat - lax.optimization_barrier(jnp.mean(flat, axis=1, keepdims=True))
    inverse_std = lax.rsqrt(lax.optimization_barrier(jnp.mean(center * center, axis=1, keepdims=True)) + 1e-05)
    return (center * inverse_std, inverse_std)

def reference(table, slot_rows, slot_counts, positions, fm_proj, ln_gain, w_up, w_down, w_lcb, cotangent):
    highest = lax.Precision.HIGHEST
    samples = positions.shape[0]
    group_rows = B_DEV * N_SHARD
    block = H // N_SHARD
    sample_ids = jnp.arange(samples, dtype=jnp.int32)[:, None]
    group_ids = sample_ids // group_rows
    member_ids = sample_ids // B_DEV % N_SHARD
    owner_ids = positions // CAP
    slot_ids = positions % CAP
    table_row = owner_ids * ROWS_DEV + slot_rows[group_ids, member_ids, owner_ids, slot_ids]
    live_mask = slot_ids < slot_counts[group_ids, member_ids, owner_ids]
    embeds = jnp.where(live_mask[:, :, None], table[table_row], jnp.zeros((), table.dtype))
    embeds_f = embeds.astype(jnp.float32)
    projector = fm_proj.astype(jnp.float32)
    compressed = jnp.einsum('bfd,fk->bdk', embeds_f, projector, precision=highest)
    gram = jnp.einsum('bfd,bdk->bfk', embeds_f, compressed, precision=highest).reshape(samples, F * K)
    normal_part, inverse_std = layer_norm(gram)
    normed = (normal_part * ln_gain).astype(jnp.bfloat16)
    preact = jnp.dot(normed, w_up, preferred_element_type=jnp.float32)
    activ = jax.nn.silu(preact).astype(jnp.bfloat16)
    activ_blocks = activ.reshape(samples, N_SHARD, block).transpose(1, 0, 2)
    mlp_out = rounded_sum(activ_blocks, w_down.reshape(N_SHARD, block, NF * D))
    lcb_weight = w_lcb.astype(jnp.float32)
    linear_part = jnp.einsum('lf,bfd->bld', lcb_weight, embeds_f, precision=highest)
    joined = jnp.concatenate([mlp_out.reshape(samples, NF, D), linear_part], axis=1)
    mixed = (embeds_f + joined).astype(jnp.bfloat16)
    grad_mlp = cotangent[:, :NF, :].reshape(samples, NF * D)
    d_hidden = jnp.dot(grad_mlp, w_down.T, preferred_element_type=jnp.float32)
    sigmoid_pre = jax.nn.sigmoid(preact)
    d_pre = (d_hidden * sigmoid_pre * (1.0 + preact * (1.0 - sigmoid_pre))).astype(jnp.bfloat16)
    grad_w_down = rounded_sum(activ.reshape(N_DP, group_rows, H).transpose(0, 2, 1), grad_mlp.reshape(N_DP, group_rows, NF * D)).astype(jnp.bfloat16)
    grad_w_up = rounded_sum(normed.reshape(N_DP, group_rows, F * K).transpose(0, 2, 1), d_pre.reshape(N_DP, group_rows, H)).astype(jnp.bfloat16)
    d_normed = rounded_sum(d_pre.reshape(samples, N_SHARD, block).transpose(1, 0, 2), w_up.reshape(F * K, N_SHARD, block).transpose(1, 2, 0))
    grad_ln_gain = lax.optimization_barrier(jnp.sum(d_normed * normal_part, axis=0))
    scaled = d_normed * ln_gain
    d_gram = inverse_std * (scaled - lax.optimization_barrier(jnp.mean(scaled, axis=1, keepdims=True)) - normal_part * lax.optimization_barrier(jnp.mean(scaled * normal_part, axis=1, keepdims=True)))
    d_gram = d_gram.reshape(samples, F, K)
    d_compressed = jnp.einsum('bfd,bfk->bdk', embeds_f, d_gram, precision=highest)
    grad_fm_proj = jnp.einsum('bfd,bdk->fk', embeds_f, d_compressed, precision=highest)
    grad_linear = cotangent[:, NF:, :].astype(jnp.float32)
    grad_w_lcb = jnp.einsum('bld,bfd->lf', grad_linear, embeds_f, precision=highest)
    d_embeds = cotangent.astype(jnp.float32)
    d_embeds = d_embeds + jnp.einsum('bfk,bdk->bfd', d_gram, compressed, precision=highest)
    d_embeds = d_embeds + jnp.einsum('fk,bdk->bfd', projector, d_compressed, precision=highest)
    d_embeds = d_embeds + jnp.einsum('lf,bld->bfd', lcb_weight, grad_linear, precision=highest)
    masked = jnp.where(live_mask[:, :, None], d_embeds, jnp.zeros((), d_embeds.dtype))
    grad_table = jax.ops.segment_sum(masked.reshape(-1, D), table_row.reshape(-1), num_segments=N_SHARD * ROWS_DEV)
    return (mixed, grad_table, grad_w_up, grad_w_down, grad_fm_proj, grad_w_lcb, grad_ln_gain)
```

```python
import jax
import jax.numpy as jnp
from jax import lax
from jax.sharding import PartitionSpec as P

F = 128
K = 8
NF = 16
CAP = 32
LANES = 128


def layer_norm(flat):
    center = flat - jnp.mean(flat, axis=1, keepdims=True)
    inverse_std = lax.rsqrt(jnp.mean(center * center, axis=1, keepdims=True) + 1e-05)
    return (center * inverse_std, inverse_std)


def exchange(blocks, axis):
    return lax.all_to_all(blocks, axis, split_axis=0, concat_axis=0, tiled=True)


def spread(block, axis):
    count = lax.axis_size(axis)
    return exchange(jnp.broadcast_to(block[None], (count, *block.shape)), axis)


def summed(blocks, axis):
    return jnp.sum(exchange(blocks, axis).astype(jnp.float32), axis=0)


def body(
    table, slot_rows, slot_counts, positions, fm_proj, ln_gain, w_up, w_down, w_lcb, cotangent
):
    highest = lax.Precision.HIGHEST
    f32, bf16 = jnp.float32, jnp.bfloat16
    members = lax.axis_size("shard")
    groups = lax.axis_size("dp")
    batch = positions.shape[0]
    width = table.shape[1]
    rows_here = table.shape[0]
    slots = members * CAP
    hidden = w_up.shape[1]
    request = slot_rows.reshape(members, CAP)
    counts_here = slot_counts.reshape(members)

    grad_mlp = cotangent[:, :NF, :].reshape(batch, NF * width)
    group_grads = lax.all_gather(grad_mlp, "shard", axis=0, tiled=True)

    asked = exchange(request, "shard").reshape(slots)
    row_ids = lax.broadcasted_iota(jnp.int32, (slots, rows_here), 1)
    asked_hot = (asked[:, None] == row_ids).astype(bf16)
    sent = jnp.dot(asked_hot, table, preferred_element_type=f32).astype(bf16)
    fetched = exchange(sent.reshape(members, CAP, width), "shard")
    live_mask = lax.broadcasted_iota(jnp.int32, (members, CAP), 1) < counts_here[:, None]
    fetched = jnp.where(live_mask[:, :, None], fetched, jnp.zeros((), bf16)).reshape(slots, width)
    flat_positions = positions.reshape(batch * F)
    slot_ids = lax.broadcasted_iota(jnp.int32, (batch * F, slots), 1)
    slot_hot = (flat_positions[:, None] == slot_ids).astype(bf16)
    embeds = jnp.dot(slot_hot, fetched, preferred_element_type=f32).astype(bf16)
    embeds = embeds.reshape(batch, F, width)

    embeds_f = embeds.astype(f32)
    projector = fm_proj.astype(f32)
    compressed = jnp.einsum("bfd,fk->bdk", embeds_f, projector, precision=highest)
    gram = jnp.einsum("bfd,bdk->bfk", embeds_f, compressed, precision=highest).reshape(batch, F * K)
    normal_part, inverse_std = layer_norm(gram)
    normed = (normal_part * ln_gain).astype(bf16)
    group_normed = spread(normed, "shard").reshape(members * batch, F * K)

    preact = jnp.dot(group_normed, w_up, preferred_element_type=f32)
    d_hidden = lax.dot_general(
        group_grads, w_down, (((1,), (1,)), ((), ())), preferred_element_type=f32
    )
    sigmoid_pre = jax.nn.sigmoid(preact)
    d_pre = (d_hidden * sigmoid_pre * (1.0 + preact * (1.0 - sigmoid_pre))).astype(bf16)
    d_normed_part = lax.dot_general(
        d_pre, w_up, (((1,), (1,)), ((), ())), preferred_element_type=f32
    ).astype(bf16)
    d_normed = summed(d_normed_part.reshape(members, batch, F * K), "shard")

    activ = jax.nn.silu(preact).astype(bf16)
    mlp_part = jnp.dot(activ, w_down, preferred_element_type=f32).astype(bf16)
    mlp_out = summed(mlp_part.reshape(members, batch, NF * width), "shard")
    down_part = lax.dot_general(
        group_grads, activ, (((0,), (0,)), ((), ())), preferred_element_type=f32
    ).astype(bf16)
    up_part = lax.dot_general(
        group_normed, d_pre, (((0,), (0,)), ((), ())), preferred_element_type=f32
    ).astype(bf16)
    down_sum = summed(down_part.reshape(groups, NF * width // groups, hidden), "dp")
    grad_w_down = down_sum.astype(bf16).T
    grad_w_up = summed(up_part.reshape(groups, F * K // groups, hidden), "dp").astype(bf16)

    grad_linear = cotangent[:, NF:, :]
    linear_part = jnp.einsum("lf,bfd->bld", w_lcb, embeds, preferred_element_type=f32)
    lcb_part = jnp.einsum("bld,bfd->lf", grad_linear, embeds, preferred_element_type=f32)
    d_linear = jnp.einsum("lf,bld->bfd", w_lcb, grad_linear, preferred_element_type=f32)

    gain_part = jnp.sum(d_normed * normal_part, axis=0)
    scaled = d_normed * ln_gain
    d_gram = inverse_std * (
        scaled
        - jnp.mean(scaled, axis=1, keepdims=True)
        - normal_part * jnp.mean(scaled * normal_part, axis=1, keepdims=True)
    )
    d_gram = d_gram.reshape(batch, F, K)
    d_compressed = jnp.einsum("bfd,bfk->bdk", embeds_f, d_gram, precision=highest)
    d_embeds = cotangent.astype(f32) + d_linear
    d_embeds = d_embeds + jnp.einsum("bfk,bdk->bfd", d_gram, compressed, precision=highest)
    d_embeds = d_embeds + jnp.einsum("fk,bdk->bfd", projector, d_compressed, precision=highest)
    d_embeds = d_embeds.astype(bf16).reshape(batch * F, width)
    slot_rows_hot = (
        lax.broadcasted_iota(jnp.int32, (slots, batch * F), 0) == flat_positions[None, :]
    ).astype(bf16)
    slot_grad = jnp.dot(slot_rows_hot, d_embeds, preferred_element_type=f32)
    slot_grad = slot_grad.reshape(members, CAP, width)
    slot_grad = jnp.where(live_mask[:, :, None], slot_grad, 0.0).astype(bf16)
    returned = exchange(slot_grad, "shard").reshape(slots, width)
    row_hot = (
        lax.broadcasted_iota(jnp.int32, (rows_here, slots), 0) == asked[None, :]
    ).astype(bf16)
    table_part = lax.dot_general(
        returned, row_hot, (((0,), (1,)), ((), ())), preferred_element_type=f32
    ).astype(bf16)
    columns = rows_here // LANES
    table_part = table_part.reshape(width, columns, LANES).transpose(1, 0, 2)
    table_sum = summed(table_part.reshape(groups, -1, LANES), "dp").astype(bf16)
    table_all = spread(table_sum, "dp").reshape(columns, width, LANES)
    grad_table = table_all.transpose(0, 2, 1).reshape(rows_here, width).astype(f32)

    proj_part = jnp.einsum("bfd,bdk->fk", embeds_f, d_compressed, precision=highest)
    small = jnp.concatenate([gain_part, proj_part.reshape(-1), lcb_part.reshape(-1)])
    small = small.reshape(members, -1, LANES)
    small = summed(small, "shard")
    small = jnp.sum(spread(small, "dp"), axis=0)
    small = spread(small, "shard").reshape(-1)
    grad_ln_gain = small[: F * K]
    grad_fm_proj = small[F * K : 2 * F * K].reshape(F, K)
    grad_w_lcb = small[2 * F * K :].reshape(F - NF, F)

    joined = jnp.concatenate([mlp_out.reshape(batch, NF, width), linear_part], axis=1)
    mixed = (embeds_f + joined).astype(bf16)
    return (mixed, grad_table, grad_w_up, grad_w_down, grad_fm_proj, grad_w_lcb, grad_ln_gain)


def solution(mesh):
    placed = (
        P("shard", None),
        P("dp", "shard", None, None),
        P("dp", "shard", None),
        P(("dp", "shard"), None),
        P(),
        P(),
        P(None, "shard"),
        P("shard", None),
        P(),
        P(("dp", "shard"), None, None),
    )
    return jax.shard_map(
        body,
        mesh=mesh,
        in_specs=placed,
        out_specs=(
            P(("dp", "shard"), None, None),
            P("shard", None),
            P("dp", "shard"),
            P("shard", "dp"),
            P(),
            P(),
            P(),
        ),
        check_vma=False,
    )
```

```python
import jax
import jax.numpy as jnp
from jax import lax
from jax.experimental import pallas as pl
from jax.experimental.pallas import tpu as pltpu
from jax.sharding import PartitionSpec as P

F = 128
K = 8
NF = 16
CAP = 32
LANES = 128


def layer_norm(flat):
    center = flat - jnp.mean(flat, axis=1, keepdims=True)
    inverse_std = lax.rsqrt(jnp.mean(center * center, axis=1, keepdims=True) + 1e-05)
    return (center * inverse_std, inverse_std)


def exchange(blocks, axis):
    return lax.all_to_all(blocks, axis, split_axis=0, concat_axis=0, tiled=True)


def spread(block, axis):
    count = lax.axis_size(axis)
    return exchange(jnp.broadcast_to(block[None], (count, *block.shape)), axis)


def gather(block, axis):
    return lax.all_gather(block, axis, axis=0, tiled=True)


def scatter(blocks, axis):
    return lax.psum_scatter(blocks, axis, scatter_dimension=0, tiled=True)


def halves(value):
    high = lax.reduce_precision(value, 8, 7)
    return jnp.concatenate([high, value - high], axis=-1).astype(jnp.bfloat16)


def network_kernel(ring, weights, lcb, back, activ, d_pre):
    f32, bf16 = jnp.float32, jnp.bfloat16
    split, end = F * K, weights.shape[1]
    cross = (((1,), (1,)), ((), ()))
    preact = lax.dot_general(
        ring[:, :split], weights[:, :split], cross, preferred_element_type=f32
    )
    d_hidden = lax.dot_general(
        ring[:, split:], weights[:, split:], cross, preferred_element_type=f32
    )
    sigmoid = 1.0 / (1.0 + jnp.exp(-preact))
    activ[...] = (preact * sigmoid).astype(bf16)
    d_pre[...] = (d_hidden * sigmoid * (1.0 + preact * (1.0 - sigmoid))).astype(bf16)
    back[:, :split] = jnp.dot(
        d_pre[...], weights[:, :split], preferred_element_type=f32
    ).astype(bf16)
    for start in range(split, end, 512):
        columns = slice(start, start + 512)
        back[:, columns] = jnp.dot(
            activ[...], weights[:, columns], preferred_element_type=f32
        ).astype(bf16)
    back[:, end:] = lcb[...]


def network(ring, weights, lcb):
    samples, taps = ring.shape[0], weights.shape[0]
    columns = weights.shape[1] + lcb.shape[1]
    return pl.pallas_call(
        network_kernel,
        out_shape=(
            jax.ShapeDtypeStruct((samples, columns), jnp.bfloat16),
            jax.ShapeDtypeStruct((samples, taps), jnp.bfloat16),
            jax.ShapeDtypeStruct((samples, taps), jnp.bfloat16),
        ),
        compiler_params=pltpu.CompilerParams(vmem_limit_bytes=32 * 2**20),
        cost_estimate=pl.CostEstimate(
            flops=4 * samples * taps * columns, bytes_accessed=6_000_000, transcendentals=65536
        ),
    )(ring, weights, lcb)


def weight_kernel(me, ring, activ, d_pre, keep, send):
    _, depth, _, _ = keep.shape
    first = me[0] == 0
    split = F * K
    start = 0
    for begin, end, right in ((split, ring.shape[1], activ), (0, split, d_pre)):
        rows = (end - begin) // (2 * depth)
        for z in range(depth):
            at = begin + z * 2 * rows
            part = lax.dot_general(
                ring[:, at : at + 2 * rows],
                right[...],
                (((0,), (0,)), ((), ())),
                preferred_element_type=jnp.float32,
            )
            low, high = part[:rows], part[rows:]
            here = slice(start, start + rows)
            keep[0, z, here] = jnp.where(first, low, high).astype(jnp.bfloat16)
            send[0, z, here] = jnp.where(first, high, low).astype(jnp.bfloat16)
        start += rows


def weight_products(ring, activ, d_pre, hidden, depth):
    samples = ring.shape[0]
    far = activ.shape[1] // hidden
    rows = ring.shape[1] // (2 * depth)
    chunk = pl.BlockSpec((samples, hidden), lambda j: (0, j))
    half = pl.BlockSpec((1, depth, rows, hidden), lambda j: (j, 0, 0, 0))
    shape = jax.ShapeDtypeStruct((far, depth, rows, hidden), jnp.bfloat16)
    return pl.pallas_call(
        weight_kernel,
        grid=(far,),
        in_specs=[
            pl.BlockSpec(memory_space=pltpu.SMEM),
            pl.BlockSpec(ring.shape, lambda j: (0, 0)),
            chunk,
            chunk,
        ],
        out_specs=(half, half),
        out_shape=(shape, shape),
        compiler_params=pltpu.CompilerParams(vmem_limit_bytes=32 * 2**20),
        cost_estimate=pl.CostEstimate(
            flops=4 * samples * rows * depth * far * hidden,
            bytes_accessed=6_000_000,
            transcendentals=0,
        ),
    )(lax.axis_index("core").reshape(1), ring, activ, d_pre)


def body(
    table, slot_rows, slot_counts, positions, fm_proj, ln_gain, w_up, w_down, w_lcb, cotangent
):
    highest = lax.Precision.HIGHEST
    f32, bf16 = jnp.float32, jnp.bfloat16
    shard, dp = ("x", "y"), ("z", "core")
    far, near = lax.axis_size("x"), lax.axis_size("y")
    depth, cores = lax.axis_size("z"), lax.axis_size("core")
    members, groups = far * near, depth * cores
    batch = positions.shape[0]
    width = table.shape[1]
    rows_here = table.shape[0]
    slots = members * CAP
    hidden = w_up.shape[1]
    request = slot_rows.reshape(members, CAP)
    counts_here = slot_counts.reshape(members)

    grad_mlp = cotangent[:, :NF, :].reshape(batch, NF * width)
    weights = gather(jnp.concatenate([w_up.T, w_down], axis=1), "x")

    asked = exchange(request, shard).reshape(slots)
    row_ids = lax.broadcasted_iota(jnp.int32, (slots, rows_here), 1)
    asked_hot = (asked[:, None] == row_ids).astype(bf16)
    sent = jnp.dot(asked_hot, table, preferred_element_type=f32).astype(bf16)
    fetched = exchange(sent.reshape(members, CAP, width), shard)
    live_mask = lax.broadcasted_iota(jnp.int32, (members, CAP), 1) < counts_here[:, None]
    fetched = jnp.where(live_mask[:, :, None], fetched, jnp.zeros((), bf16)).reshape(slots, width)
    flat_positions = positions.reshape(batch * F)
    slot_ids = lax.broadcasted_iota(jnp.int32, (batch * F, slots), 1)
    slot_hot = (flat_positions[:, None] == slot_ids).astype(bf16)
    embeds = jnp.dot(slot_hot, fetched, preferred_element_type=f32).astype(bf16)
    embeds = embeds.reshape(batch, F, width)

    embeds_f = embeds.astype(f32)
    projector = fm_proj.astype(f32)
    compressed = jnp.einsum("bfd,fk->bdk", embeds, fm_proj, preferred_element_type=f32)
    gram = jnp.einsum("bfd,bdk->bfk", embeds_f, compressed, precision=highest).reshape(batch, F * K)
    normal_part, inverse_std = layer_norm(gram)
    normed = (normal_part * ln_gain).astype(bf16)
    ring = spread(jnp.concatenate([normed, grad_mlp], axis=1), "y")
    ring = ring.reshape(near * batch, -1)

    grad_linear = cotangent[:, NF:, :]
    linear_part = jnp.einsum("lf,bfd->bld", w_lcb, embeds, preferred_element_type=f32)
    lcb_part = jnp.einsum("bld,bfd->lf", grad_linear, embeds, preferred_element_type=f32)
    lcb_part = lcb_part.astype(bf16).reshape(near * batch, -1)
    spare = -lcb_part.shape[1] % LANES
    back, activ, d_pre = network(ring, weights, jnp.pad(lcb_part, ((0, 0), (0, spare))))
    back = exchange(back.reshape(near, batch, -1), "y")
    keep, send = weight_products(ring, activ, d_pre, hidden, depth)
    other = lax.ppermute(send, "core", [(0, 1), (1, 0)])
    weight_sum = (keep.astype(f32) + other.astype(f32)).astype(bf16).reshape(-1, hidden)
    back, weight_sum = lax.optimization_barrier((back, weight_sum))
    weight_sum = scatter(weight_sum, "x")
    back = jnp.sum(back.astype(f32), axis=0)
    split, end = F * K, F * K + NF * width
    d_normed, mlp_out = back[:, :split], back[:, split:end]
    lcb_mine = back[:, end : end + lcb_part.shape[1]].astype(bf16)
    d_linear = jnp.einsum("lf,bld->bfd", w_lcb, grad_linear, preferred_element_type=f32)

    gain_part = jnp.sum(d_normed * normal_part, axis=0)
    scaled = d_normed * ln_gain
    d_gram = inverse_std * (
        scaled
        - jnp.mean(scaled, axis=1, keepdims=True)
        - normal_part * jnp.mean(scaled * normal_part, axis=1, keepdims=True)
    )
    d_gram = d_gram.reshape(batch, F, K)
    d_compressed = jnp.einsum("bfd,bfk->bdk", embeds_f, d_gram, precision=highest)
    d_embeds = cotangent.astype(f32) + d_linear
    d_embeds = d_embeds + jnp.einsum("bfk,bdk->bfd", d_gram, compressed, precision=highest)
    d_embeds = d_embeds + jnp.einsum("fk,bdk->bfd", projector, d_compressed, precision=highest)
    d_embeds = d_embeds.astype(bf16).reshape(batch * F, width)
    slot_rows_hot = (
        lax.broadcasted_iota(jnp.int32, (slots, batch * F), 0) == flat_positions[None, :]
    ).astype(bf16)
    slot_grad = jnp.dot(slot_rows_hot, d_embeds, preferred_element_type=f32)
    slot_grad = slot_grad.reshape(members, CAP, width)
    slot_grad = jnp.where(live_mask[:, :, None], slot_grad, 0.0).astype(bf16)
    proj_part = jnp.einsum("bfd,bdk->fk", embeds, halves(d_compressed), preferred_element_type=f32)
    proj_part = proj_part[:, :K] + proj_part[:, K:]
    small = jnp.concatenate([gain_part, proj_part.reshape(-1)]).astype(bf16).reshape(CAP, -1)
    row = 2 * LANES
    lcb_mine = lcb_mine.reshape(-1, row)
    lcb_mine = jnp.pad(lcb_mine, ((0, -lcb_mine.shape[0] % 8), (0, 0)))
    small = jnp.pad(small, ((0, 0), (0, row - width - small.shape[1])))
    sent = jnp.concatenate([slot_grad, jnp.broadcast_to(small[None], (members, *small.shape))], axis=2)
    lcb_sent = jnp.broadcast_to(lcb_mine[None], (members, *lcb_mine.shape))
    received = exchange(jnp.concatenate([sent, lcb_sent], axis=1), shard)
    received, weight_sum = lax.optimization_barrier((received, weight_sum))
    weight_sum = scatter(weight_sum, "z")
    returned = received[:, :CAP, :width].reshape(slots, width)
    small_end = width + 2 * F * K // CAP
    small = jnp.sum(received[:, :CAP, width:small_end].astype(f32), axis=0).astype(bf16)
    lcb = received[:, CAP:].reshape(far, near, -1)[:, :, : (F - NF) * F // near]
    lcb = jnp.sum(lcb.astype(f32), axis=0).astype(bf16)
    small = jnp.concatenate([small.reshape(-1), lcb.reshape(-1)]).reshape(groups, -1, LANES)
    row_hot = (
        lax.broadcasted_iota(jnp.int32, (rows_here, slots), 0) == asked[None, :]
    ).astype(bf16)
    table_part = lax.dot_general(
        returned, row_hot, (((0,), (1,)), ((), ())), preferred_element_type=f32
    ).astype(bf16)
    columns = rows_here // LANES
    table_part = table_part.reshape(width, columns, LANES).transpose(1, 0, 2)
    table_part = table_part.reshape(groups, -1, LANES)
    held = table_part.shape[1]
    total = exchange(jnp.concatenate([table_part, small], axis=1), dp)
    total = spread(jnp.sum(total.astype(f32), axis=0).astype(bf16), dp)
    total, weight_sum = lax.optimization_barrier((total, weight_sum))
    down_count = NF * width // groups
    grad_w_down = weight_sum[:down_count].T
    grad_w_up = weight_sum[down_count:]
    table_all = total[:, :held].reshape(columns, width, LANES)
    grad_table = table_all.transpose(0, 2, 1).reshape(rows_here, width).astype(f32)
    small = total[:, held:].reshape(-1).astype(f32)
    grad_ln_gain = small[: F * K]
    grad_fm_proj = small[F * K : 2 * F * K].reshape(F, K)
    grad_w_lcb = small[2 * F * K :].reshape(F - NF, F)

    joined = jnp.concatenate([mlp_out.reshape(batch, NF, width), linear_part], axis=1)
    mixed = (embeds_f + joined).astype(bf16)
    return (mixed, grad_table, grad_w_up, grad_w_down, grad_fm_proj, grad_w_lcb, grad_ln_gain)


def solution(mesh):
    dp, shard = mesh.devices.shape
    near = min(8, shard // 2)
    split = (dp // 2, 2, shard // near, near)
    mesh = jax.sharding.Mesh(mesh.devices.reshape(split), ("z", "core", "x", "y"))
    dp, shard = ("z", "core"), ("x", "y")
    every = (*dp, *shard)
    placed = (
        P(shard, None),
        P(dp, shard, None, None),
        P(dp, shard, None),
        P(every, None),
        P(),
        P(),
        P(None, shard),
        P(shard, None),
        P(),
        P(every, None, None),
    )
    return jax.shard_map(
        body,
        mesh=mesh,
        in_specs=placed,
        out_specs=(
            P(every, None, None),
            P(shard, None),
            P(dp, shard),
            P(shard, dp),
            P(),
            P(),
            P(),
        ),
        check_vma=False,
    )
```

```python
import jax
import jax.numpy as jnp
from jax import lax
from jax.experimental import pallas as pl
from jax.experimental.pallas import tpu as pltpu
from jax.sharding import PartitionSpec as P

F = 128
K = 8
NF = 16
CAP = 32
LANES = 128


def layer_norm(flat):
    center = flat - jnp.mean(flat, axis=1, keepdims=True)
    inverse_std = lax.rsqrt(jnp.mean(center * center, axis=1, keepdims=True) + 1e-05)
    return (center * inverse_std, inverse_std)


def exchange(blocks, axis):
    return lax.all_to_all(blocks, axis, split_axis=0, concat_axis=0, tiled=True)


def spread(block, axis):
    count = lax.axis_size(axis)
    return exchange(jnp.broadcast_to(block[None], (count, *block.shape)), axis)


def gather(block, axis):
    return lax.all_gather(block, axis, axis=0, tiled=True)


def scatter(blocks, axis):
    return lax.psum_scatter(blocks, axis, scatter_dimension=0, tiled=True)


def halves(value):
    high = lax.reduce_precision(value, 8, 7)
    return jnp.concatenate([high, value - high], axis=-1).astype(jnp.bfloat16)


def network_kernel(ring, weights, lcb, back, mlp, activ, d_pre):
    f32, bf16 = jnp.float32, jnp.bfloat16
    split, end = F * K, weights.shape[1]
    cross = (((1,), (1,)), ((), ()))
    preact = lax.dot_general(
        ring[:, :split], weights[:, :split], cross, preferred_element_type=f32
    )
    d_hidden = lax.dot_general(
        ring[:, split:], weights[:, split:], cross, preferred_element_type=f32
    )
    sigmoid = 1.0 / (1.0 + jnp.exp(-preact))
    activ[...] = (preact * sigmoid).astype(bf16)
    d_pre[...] = (d_hidden * sigmoid * (1.0 + preact * (1.0 - sigmoid))).astype(bf16)
    back[...] = jnp.dot(d_pre[...], weights[:, :split], preferred_element_type=f32).astype(bf16)
    for start in range(0, end - split, 512):
        mlp[:, start : start + 512] = jnp.dot(
            activ[...],
            weights[:, split + start : split + start + 512],
            preferred_element_type=f32,
        ).astype(bf16)
    mlp[:, end - split :] = lcb[...]


def network(ring, weights, lcb):
    samples, taps = ring.shape[0], weights.shape[0]
    columns = weights.shape[1] + lcb.shape[1]
    return pl.pallas_call(
        network_kernel,
        out_shape=(
            jax.ShapeDtypeStruct((samples, F * K), jnp.bfloat16),
            jax.ShapeDtypeStruct((samples, columns - F * K), jnp.bfloat16),
            jax.ShapeDtypeStruct((samples, taps), jnp.bfloat16),
            jax.ShapeDtypeStruct((samples, taps), jnp.bfloat16),
        ),
        compiler_params=pltpu.CompilerParams(vmem_limit_bytes=32 * 2**20),
        cost_estimate=pl.CostEstimate(
            flops=4 * samples * taps * columns, bytes_accessed=6_000_000, transcendentals=65536
        ),
    )(ring, weights, lcb)


def weight_kernel(me, ring, activ, d_pre, keep, send):
    _, depth, _, _ = keep.shape
    first = me[0] == 0
    split = F * K
    start = 0
    for begin, end, right in ((split, ring.shape[1], activ), (0, split, d_pre)):
        rows = (end - begin) // (2 * depth)
        for z in range(depth):
            at = begin + z * 2 * rows
            part = lax.dot_general(
                ring[:, at : at + 2 * rows],
                right[...],
                (((0,), (0,)), ((), ())),
                preferred_element_type=jnp.float32,
            )
            low, high = part[:rows], part[rows:]
            here = slice(start, start + rows)
            keep[0, z, here] = jnp.where(first, low, high).astype(jnp.bfloat16)
            send[0, z, here] = jnp.where(first, high, low).astype(jnp.bfloat16)
        start += rows


def weight_products(ring, activ, d_pre, hidden, depth):
    samples = ring.shape[0]
    far = activ.shape[1] // hidden
    rows = ring.shape[1] // (2 * depth)
    chunk = pl.BlockSpec((samples, hidden), lambda j: (0, j))
    half = pl.BlockSpec((1, depth, rows, hidden), lambda j: (j, 0, 0, 0))
    shape = jax.ShapeDtypeStruct((far, depth, rows, hidden), jnp.bfloat16)
    return pl.pallas_call(
        weight_kernel,
        grid=(far,),
        in_specs=[
            pl.BlockSpec(memory_space=pltpu.SMEM),
            pl.BlockSpec(ring.shape, lambda j: (0, 0)),
            chunk,
            chunk,
        ],
        out_specs=(half, half),
        out_shape=(shape, shape),
        compiler_params=pltpu.CompilerParams(vmem_limit_bytes=32 * 2**20),
        cost_estimate=pl.CostEstimate(
            flops=4 * samples * rows * depth * far * hidden,
            bytes_accessed=6_000_000,
            transcendentals=0,
        ),
    )(lax.axis_index("core").reshape(1), ring, activ, d_pre)


def body(
    table, slot_rows, slot_counts, positions, fm_proj, ln_gain, w_up, w_down, w_lcb, cotangent
):
    highest = lax.Precision.HIGHEST
    f32, bf16 = jnp.float32, jnp.bfloat16
    shard, dp = ("x", "y"), ("zh", "zl", "core")
    far, near = lax.axis_size("x"), lax.axis_size("y")
    depth = lax.axis_size("zh") * lax.axis_size("zl")
    members, groups = far * near, depth * lax.axis_size("core")
    batch = positions.shape[0]
    width = table.shape[1]
    rows_here = table.shape[0]
    slots = members * CAP
    hidden = w_up.shape[1]
    request = slot_rows.reshape(members, CAP)
    counts_here = slot_counts.reshape(members)

    grad_mlp = cotangent[:, :NF, :].reshape(batch, NF * width)
    weights = gather(jnp.concatenate([w_up.T, w_down], axis=1), "x")

    asked = exchange(request, shard).reshape(slots)
    row_ids = lax.broadcasted_iota(jnp.int32, (slots, rows_here), 1)
    asked_hot = (asked[:, None] == row_ids).astype(bf16)
    sent = jnp.dot(asked_hot, table, preferred_element_type=f32).astype(bf16)
    fetched = exchange(sent.reshape(members, CAP, width), shard)
    live_mask = lax.broadcasted_iota(jnp.int32, (members, CAP), 1) < counts_here[:, None]
    fetched = jnp.where(live_mask[:, :, None], fetched, jnp.zeros((), bf16)).reshape(slots, width)
    flat_positions = positions.reshape(batch * F)
    slot_ids = lax.broadcasted_iota(jnp.int32, (batch * F, slots), 1)
    slot_hot = (flat_positions[:, None] == slot_ids).astype(bf16)
    embeds = jnp.dot(slot_hot, fetched, preferred_element_type=f32).astype(bf16)
    embeds = embeds.reshape(batch, F, width)

    embeds_f = embeds.astype(f32)
    projector = fm_proj.astype(f32)
    compressed = jnp.einsum("bfd,fk->bdk", embeds, fm_proj, preferred_element_type=f32)
    gram = jnp.einsum("bfd,bdk->bfk", embeds_f, compressed, precision=highest).reshape(batch, F * K)
    normal_part, inverse_std = layer_norm(gram)
    normed = (normal_part * ln_gain).astype(bf16)
    ring = spread(jnp.concatenate([normed, grad_mlp], axis=1), "y")
    ring = ring.reshape(near * batch, -1)

    grad_linear = cotangent[:, NF:, :]
    linear_part = jnp.einsum("lf,bfd->bld", w_lcb, embeds, preferred_element_type=f32)
    lcb_part = jnp.einsum("bld,bfd->lf", grad_linear, embeds, preferred_element_type=f32)
    lcb_part = lcb_part.astype(bf16).reshape(near * batch, -1)
    spare = -lcb_part.shape[1] % LANES
    lcb_padded = jnp.pad(lcb_part, ((0, 0), (0, spare)))
    back, mlp_part, activ, d_pre = network(ring, weights, lcb_padded)
    d_normed = exchange(back.reshape(near, batch, -1), "y")
    keep, send = weight_products(ring, activ, d_pre, hidden, depth)
    other = lax.ppermute(send, "core", [(0, 1), (1, 0)])
    weight_sum = (keep.astype(f32) + other.astype(f32)).astype(bf16).reshape(-1, hidden)
    d_normed, mlp_part, _ = lax.optimization_barrier((d_normed, mlp_part, weight_sum))
    weight_sum = scatter(weight_sum, "x")
    d_normed = jnp.sum(d_normed.astype(f32), axis=0)
    mlp_sum = jnp.sum(exchange(mlp_part.reshape(near, batch, -1), "y").astype(f32), axis=0)
    end = NF * width
    mlp_out = mlp_sum[:, :end]
    lcb_mine = mlp_sum[:, end : end + lcb_part.shape[1]].astype(bf16)
    d_linear = jnp.einsum("lf,bld->bfd", w_lcb, grad_linear, preferred_element_type=f32)

    gain_part = jnp.sum(d_normed * normal_part, axis=0)
    scaled = d_normed * ln_gain
    d_gram = inverse_std * (
        scaled
        - jnp.mean(scaled, axis=1, keepdims=True)
        - normal_part * jnp.mean(scaled * normal_part, axis=1, keepdims=True)
    )
    d_gram = d_gram.reshape(batch, F, K)
    d_compressed = jnp.einsum("bfd,bfk->bdk", embeds_f, d_gram, precision=highest)
    d_embeds = cotangent.astype(f32) + d_linear
    d_embeds = d_embeds + jnp.einsum("bfk,bdk->bfd", d_gram, compressed, precision=highest)
    d_embeds = d_embeds + jnp.einsum("fk,bdk->bfd", projector, d_compressed, precision=highest)
    d_embeds = d_embeds.astype(bf16).reshape(batch * F, width)
    slot_rows_hot = (
        lax.broadcasted_iota(jnp.int32, (slots, batch * F), 0) == flat_positions[None, :]
    ).astype(bf16)
    slot_grad = jnp.dot(slot_rows_hot, d_embeds, preferred_element_type=f32)
    slot_grad = slot_grad.reshape(members, CAP, width)
    slot_grad = jnp.where(live_mask[:, :, None], slot_grad, 0.0).astype(bf16)
    slot_grad, weight_sum = lax.optimization_barrier((slot_grad, weight_sum))
    weight_sum = scatter(weight_sum, "zh")
    proj_part = jnp.einsum("bfd,bdk->fk", embeds, halves(d_compressed), preferred_element_type=f32)
    proj_part = proj_part[:, :K] + proj_part[:, K:]
    small = jnp.concatenate([gain_part, proj_part.reshape(-1)]).astype(bf16).reshape(CAP, -1)
    row = 2 * LANES
    lcb_mine = lcb_mine.reshape(-1, row)
    lcb_mine = jnp.pad(lcb_mine, ((0, -lcb_mine.shape[0] % 8), (0, 0)))
    small = jnp.pad(small, ((0, 0), (0, row - width - small.shape[1])))
    sent = jnp.concatenate([slot_grad, jnp.broadcast_to(small[None], (members, *small.shape))], axis=2)
    lcb_sent = jnp.broadcast_to(lcb_mine[None], (members, *lcb_mine.shape))
    received = exchange(jnp.concatenate([sent, lcb_sent], axis=1), shard)
    received, weight_sum = lax.optimization_barrier((received, weight_sum))
    weight_sum = scatter(weight_sum, "zl")
    returned = received[:, :CAP, :width].reshape(slots, width)
    small_end = width + 2 * F * K // CAP
    small = jnp.sum(received[:, :CAP, width:small_end].astype(f32), axis=0).astype(bf16)
    lcb = received[:, CAP:].reshape(far, near, -1)[:, :, : (F - NF) * F // near]
    lcb = jnp.sum(lcb.astype(f32), axis=0).astype(bf16)
    small = jnp.concatenate([small.reshape(-1), lcb.reshape(-1)]).reshape(groups, -1, LANES)
    row_hot = (
        lax.broadcasted_iota(jnp.int32, (rows_here, slots), 0) == asked[None, :]
    ).astype(bf16)
    table_part = lax.dot_general(
        returned, row_hot, (((0,), (1,)), ((), ())), preferred_element_type=f32
    ).astype(bf16)
    columns = rows_here // LANES
    table_part = table_part.reshape(width, columns, LANES).transpose(1, 0, 2)
    table_part = table_part.reshape(groups, -1, LANES)
    held = table_part.shape[1]
    total = exchange(jnp.concatenate([table_part, small], axis=1), dp)
    total = jnp.sum(total.astype(f32), axis=0).astype(bf16)
    total, weight_sum = lax.optimization_barrier((total, weight_sum))
    total = spread(total, dp)
    down_count = NF * width // groups
    grad_w_down = weight_sum[:down_count].T
    grad_w_up = weight_sum[down_count:]
    table_all = total[:, :held].reshape(columns, width, LANES)
    grad_table = table_all.transpose(0, 2, 1).reshape(rows_here, width).astype(f32)
    small = total[:, held:].reshape(-1).astype(f32)
    grad_ln_gain = small[: F * K]
    grad_fm_proj = small[F * K : 2 * F * K].reshape(F, K)
    grad_w_lcb = small[2 * F * K :].reshape(F - NF, F)

    joined = jnp.concatenate([mlp_out.reshape(batch, NF, width), linear_part], axis=1)
    mixed = (embeds_f + joined).astype(bf16)
    return (mixed, grad_table, grad_w_up, grad_w_down, grad_fm_proj, grad_w_lcb, grad_ln_gain)


def solution(mesh):
    dp, shard = mesh.devices.shape
    near = min(8, shard // 2)
    low = 2 if dp % 4 == 0 else 1
    split = (dp // 2 // low, low, 2, shard // near, near)
    dp, shard = ("zh", "zl", "core"), ("x", "y")
    mesh = jax.sharding.Mesh(mesh.devices.reshape(split), (*dp, *shard))
    every = (*dp, *shard)
    placed = (
        P(shard, None),
        P(dp, shard, None, None),
        P(dp, shard, None),
        P(every, None),
        P(),
        P(),
        P(None, shard),
        P(shard, None),
        P(),
        P(every, None, None),
    )
    return jax.shard_map(
        body,
        mesh=mesh,
        in_specs=placed,
        out_specs=(
            P(every, None, None),
            P(shard, None),
            P(dp, shard),
            P(shard, dp),
            P(),
            P(),
            P(),
        ),
        check_vma=False,
    )
```

```python
import functools

import jax
import jax.numpy as jnp
from jax import lax
from jax.experimental import pallas as pl
from jax.experimental.pallas import tpu as pltpu
from jax.sharding import PartitionSpec as P

F = 128
K = 8
NF = 16
CAP = 32
LANES = 128


def layer_norm(flat):
    center = flat - jnp.mean(flat, axis=1, keepdims=True)
    inverse_std = lax.rsqrt(jnp.mean(center * center, axis=1, keepdims=True) + 1e-05)
    return (center * inverse_std, inverse_std)


def exchange(blocks, axis):
    return lax.all_to_all(blocks, axis, split_axis=0, concat_axis=0, tiled=True)


def spread(block, axis):
    count = lax.axis_size(axis)
    return exchange(jnp.broadcast_to(block[None], (count, *block.shape)), axis)


def gather(block, axis):
    return lax.all_gather(block, axis, axis=0, tiled=True)


def scatter(blocks, axis):
    return lax.psum_scatter(blocks, axis, scatter_dimension=0, tiled=True)


def halves(value):
    high = lax.reduce_precision(value, 8, 7)
    return jnp.concatenate([high, value - high], axis=-1).astype(jnp.bfloat16)


def halved(blocks, axis, step):
    half = blocks.shape[0] // 2
    pairs = [(i, i ^ step) for i in range(lax.axis_size(axis))]
    other = lax.ppermute(blocks[half:], axis, pairs)
    return (blocks[:half].astype(jnp.float32) + other.astype(jnp.float32)).astype(jnp.bfloat16)


def network_kernel(batch, me, ring, weights, lcb, back, mlp, mine, shuffled):
    f32, bf16 = jnp.float32, jnp.bfloat16
    samples, columns = ring.shape
    split, taps = F * K, weights.shape[0]
    cross = (((1,), (1,)), ((), ()))
    preact = lax.dot_general(
        ring[:, :split], weights[:, :split], cross, preferred_element_type=f32
    )
    d_hidden = lax.dot_general(
        ring[:, split:], weights[:, split:], cross, preferred_element_type=f32
    )
    sigmoid = 1.0 / (1.0 + jnp.exp(-preact))
    activ = (preact * sigmoid).astype(bf16)
    d_pre = (d_hidden * sigmoid * (1.0 + preact * (1.0 - sigmoid))).astype(bf16)
    mine[:, :columns] = ring[...]
    mine[:, columns : columns + taps] = activ
    mine[:, columns + taps :] = d_pre
    back[:, :split] = jnp.dot(d_pre, weights[:, :split], preferred_element_type=f32).astype(bf16)
    back[:, split:] = lcb[...]
    for block in range(samples // batch):
        start = pl.multiple_of((me[0] ^ block) * batch, batch)
        shuffled[pl.ds(start, batch), :] = activ[block * batch : (block + 1) * batch]
    for start in range(0, columns - split, 512):
        mlp[:, start : start + 512] = jnp.dot(
            shuffled[...],
            weights[:, split + start : split + start + 512],
            preferred_element_type=f32,
        ).astype(bf16)


def network(ring, weights, lcb, batch):
    samples, columns = ring.shape
    taps = weights.shape[0]
    vmem = pl.BlockSpec(memory_space=pltpu.VMEM)
    shape = lambda width: jax.ShapeDtypeStruct((samples, width), jnp.bfloat16)
    return pl.pallas_call(
        functools.partial(network_kernel, batch),
        in_specs=[pl.BlockSpec(memory_space=pltpu.SMEM), vmem, vmem, vmem],
        out_shape=(shape(F * K + lcb.shape[1]), shape(columns - F * K), shape(columns + 2 * taps)),
        scratch_shapes=[pltpu.VMEM((samples, taps), jnp.bfloat16)],
        compiler_params=pltpu.CompilerParams(vmem_limit_bytes=32 * 2**20),
        cost_estimate=pl.CostEstimate(
            flops=4 * samples * taps * columns, bytes_accessed=7_000_000, transcendentals=65536
        ),
    )(lax.axis_index("y").reshape(1), ring, weights, lcb)


def weight_kernel(me, mine, other, activ, activ_other, d_pre, d_pre_other, out):
    _, depth, _, _ = out.shape
    f32 = jnp.float32
    along = (((0,), (0,)), ((), ()))
    first = me[0] == 0
    split, columns = F * K, mine.shape[1]
    start = 0
    for begin, end, right, right_other in (
        (split, columns, activ, activ_other),
        (0, split, d_pre, d_pre_other),
    ):
        rows = (end - begin) // (2 * depth)
        for z in range(depth):
            at = slice(begin + z * 2 * rows, begin + (z + 1) * 2 * rows)
            part = lax.dot_general(mine[:, at], right[...], along, preferred_element_type=f32)
            part = part + lax.dot_general(
                other[:, at], right_other[...], along, preferred_element_type=f32
            )
            part = jnp.where(first, part[:rows], part[rows:])
            out[0, z, start : start + rows] = part.astype(jnp.bfloat16)
        start += rows


def weight_products(mine, other, hidden, far, depth):
    samples = mine.shape[0]
    columns = mine.shape[1] - 2 * far * hidden
    rows = columns // (2 * depth)
    first = columns // hidden
    ring = pl.BlockSpec((samples, columns), lambda j: (0, 0))
    activ = pl.BlockSpec((samples, hidden), lambda j: (0, first + j))
    d_pre = pl.BlockSpec((samples, hidden), lambda j: (0, first + far + j))
    return pl.pallas_call(
        weight_kernel,
        grid=(far,),
        in_specs=[
            pl.BlockSpec(memory_space=pltpu.SMEM), ring, ring, activ, activ, d_pre, d_pre
        ],
        out_specs=pl.BlockSpec((1, depth, rows, hidden), lambda j: (j, 0, 0, 0)),
        out_shape=jax.ShapeDtypeStruct((far, depth, rows, hidden), jnp.bfloat16),
        compiler_params=pltpu.CompilerParams(vmem_limit_bytes=32 * 2**20),
        cost_estimate=pl.CostEstimate(
            flops=8 * samples * rows * depth * far * hidden,
            bytes_accessed=6_000_000,
            transcendentals=0,
        ),
    )(lax.axis_index("core").reshape(1), mine, other, mine, other, mine, other)


def body(
    table, slot_rows, slot_counts, positions, fm_proj, ln_gain, w_up, w_down, w_lcb, cotangent
):
    highest = lax.Precision.HIGHEST
    f32, bf16 = jnp.float32, jnp.bfloat16
    shard, dp = ("x", "y"), ("z", "core")
    far, near = lax.axis_size("x"), lax.axis_size("y")
    depth = lax.axis_size("z")
    members, groups = far * near, depth * lax.axis_size("core")
    batch = positions.shape[0]
    width = table.shape[1]
    rows_here = table.shape[0]
    slots = members * CAP
    hidden = w_up.shape[1]
    request = slot_rows.reshape(members, CAP)
    counts_here = slot_counts.reshape(members)

    grad_mlp = cotangent[:, :NF, :].reshape(batch, NF * width)
    weights = gather(jnp.concatenate([w_up.T, w_down], axis=1), "x")

    asked = exchange(request, shard).reshape(slots)
    row_ids = lax.broadcasted_iota(jnp.int32, (slots, rows_here), 1)
    asked_hot = (asked[:, None] == row_ids).astype(bf16)
    sent = jnp.dot(asked_hot, table, preferred_element_type=f32).astype(bf16)
    fetched = exchange(sent.reshape(members, CAP, width), shard)
    live_mask = lax.broadcasted_iota(jnp.int32, (members, CAP), 1) < counts_here[:, None]
    fetched = jnp.where(live_mask[:, :, None], fetched, jnp.zeros((), bf16)).reshape(slots, width)
    flat_positions = positions.reshape(batch * F)
    slot_ids = lax.broadcasted_iota(jnp.int32, (batch * F, slots), 1)
    slot_hot = (flat_positions[:, None] == slot_ids).astype(bf16)
    embeds = jnp.dot(slot_hot, fetched, preferred_element_type=f32).astype(bf16)
    embeds = embeds.reshape(batch, F, width)

    embeds_f = embeds.astype(f32)
    projector = fm_proj.astype(f32)
    compressed = jnp.einsum("bfd,fk->bdk", embeds, fm_proj, preferred_element_type=f32)
    gram = jnp.einsum("bfd,bdk->bfk", embeds_f, compressed, precision=highest).reshape(batch, F * K)
    normal_part, inverse_std = layer_norm(gram)
    normed = (normal_part * ln_gain).astype(bf16)
    ring = spread(jnp.concatenate([normed, grad_mlp], axis=1), "y")
    ring = ring.reshape(near * batch, -1)

    grad_linear = cotangent[:, NF:, :]
    linear_part = jnp.einsum("lf,bfd->bld", w_lcb, embeds, preferred_element_type=f32)
    lcb_part = jnp.einsum("bld,bfd->lf", grad_linear, embeds, preferred_element_type=f32)
    lcb_part = lcb_part.astype(bf16).reshape(near * batch, -1)
    spare = -lcb_part.shape[1] % LANES
    lcb_padded = jnp.pad(lcb_part, ((0, 0), (0, spare)))
    back, mlp_part, mine = network(ring, weights, lcb_padded, batch)
    back = exchange(back.reshape(near, batch, -1), "y")
    other = lax.ppermute(mine, "core", [(0, 1), (1, 0)])
    weight_sum = weight_products(mine, other, hidden, far, depth).reshape(-1, hidden)
    back, _ = lax.optimization_barrier((back, weight_sum))
    weight_sum = scatter(weight_sum, "x")
    back = jnp.sum(back.astype(f32), axis=0)
    d_normed = back[:, : F * K]
    lcb_mine = back[:, F * K : F * K + lcb_part.shape[1]].astype(bf16)
    d_linear = jnp.einsum("lf,bld->bfd", w_lcb, grad_linear, preferred_element_type=f32)

    gain_part = jnp.sum(d_normed * normal_part, axis=0)
    scaled = d_normed * ln_gain
    d_gram = inverse_std * (
        scaled
        - jnp.mean(scaled, axis=1, keepdims=True)
        - normal_part * jnp.mean(scaled * normal_part, axis=1, keepdims=True)
    )
    d_gram = d_gram.reshape(batch, F, K)
    d_compressed = jnp.einsum("bfd,bfk->bdk", embeds_f, d_gram, precision=highest)
    d_embeds = cotangent.astype(f32) + d_linear
    d_embeds = d_embeds + jnp.einsum("bfk,bdk->bfd", d_gram, compressed, precision=highest)
    d_embeds = d_embeds + jnp.einsum("fk,bdk->bfd", projector, d_compressed, precision=highest)
    d_embeds = d_embeds.astype(bf16).reshape(batch * F, width)
    slot_rows_hot = (
        lax.broadcasted_iota(jnp.int32, (slots, batch * F), 0) == flat_positions[None, :]
    ).astype(bf16)
    slot_grad = jnp.dot(slot_rows_hot, d_embeds, preferred_element_type=f32)
    slot_grad = slot_grad.reshape(members, CAP, width)
    slot_grad = jnp.where(live_mask[:, :, None], slot_grad, 0.0).astype(bf16)
    slot_grad, mlp_part = lax.optimization_barrier((slot_grad, mlp_part))
    mlp_part = halved(mlp_part, "y", near // 2)
    step = near // 4
    while step:
        mlp_part = halved(mlp_part, "y", step)
        step //= 2
    mlp_out = mlp_part.astype(f32)
    proj_part = jnp.einsum("bfd,bdk->fk", embeds, halves(d_compressed), preferred_element_type=f32)
    proj_part = proj_part[:, :K] + proj_part[:, K:]
    small = jnp.concatenate([gain_part, proj_part.reshape(-1)]).astype(bf16).reshape(CAP, -1)
    row = 2 * LANES
    lcb_mine = lcb_mine.reshape(-1, row)
    lcb_mine = jnp.pad(lcb_mine, ((0, -lcb_mine.shape[0] % 8), (0, 0)))
    small = jnp.pad(small, ((0, 0), (0, row - width - small.shape[1])))
    sent = jnp.concatenate([slot_grad, jnp.broadcast_to(small[None], (members, *small.shape))], axis=2)
    lcb_sent = jnp.broadcast_to(lcb_mine[None], (members, *lcb_mine.shape))
    received = exchange(jnp.concatenate([sent, lcb_sent], axis=1), shard)
    received, weight_sum = lax.optimization_barrier((received, weight_sum))
    weight_sum = scatter(weight_sum, "z")
    returned = received[:, :CAP, :width].reshape(slots, width)
    small_end = width + 2 * F * K // CAP
    small = jnp.sum(received[:, :CAP, width:small_end].astype(f32), axis=0).astype(bf16)
    lcb = received[:, CAP:].reshape(far, near, -1)[:, :, : (F - NF) * F // near]
    lcb = jnp.sum(lcb.astype(f32), axis=0).astype(bf16)
    small = jnp.concatenate([small.reshape(-1), lcb.reshape(-1)]).reshape(groups, -1, LANES)
    row_hot = (
        lax.broadcasted_iota(jnp.int32, (rows_here, slots), 0) == asked[None, :]
    ).astype(bf16)
    table_part = lax.dot_general(
        returned, row_hot, (((0,), (1,)), ((), ())), preferred_element_type=f32
    ).astype(bf16)
    columns = rows_here // LANES
    table_part = table_part.reshape(width, columns, LANES).transpose(1, 0, 2)
    table_part = table_part.reshape(groups, -1, LANES)
    held = table_part.shape[1]
    total = exchange(jnp.concatenate([table_part, small], axis=1), dp)
    total = jnp.sum(total.astype(f32), axis=0).astype(bf16)
    total, mlp_out = lax.optimization_barrier((total, mlp_out))
    total = spread(total, dp)
    total, weight_sum = lax.optimization_barrier((total, weight_sum))
    down_count = NF * width // groups
    grad_w_down = weight_sum[:down_count].T
    grad_w_up = weight_sum[down_count:]
    table_all = total[:, :held].reshape(columns, width, LANES)
    grad_table = table_all.transpose(0, 2, 1).reshape(rows_here, width).astype(f32)
    small = total[:, held:].reshape(-1).astype(f32)
    grad_ln_gain = small[: F * K]
    grad_fm_proj = small[F * K : 2 * F * K].reshape(F, K)
    grad_w_lcb = small[2 * F * K :].reshape(F - NF, F)

    joined = jnp.concatenate([mlp_out.reshape(batch, NF, width), linear_part], axis=1)
    mixed = (embeds_f + joined).astype(bf16)
    return (mixed, grad_table, grad_w_up, grad_w_down, grad_fm_proj, grad_w_lcb, grad_ln_gain)


def solution(mesh):
    dp, shard = mesh.devices.shape
    near = min(8, shard // 2)
    split = (dp // 2, 2, shard // near, near)
    dp, shard = ("z", "core"), ("x", "y")
    mesh = jax.sharding.Mesh(mesh.devices.reshape(split), (*dp, *shard))
    every = (*dp, *shard)
    placed = (
        P(shard, None),
        P(dp, shard, None, None),
        P(dp, shard, None),
        P(every, None),
        P(),
        P(),
        P(None, shard),
        P(shard, None),
        P(),
        P(every, None, None),
    )
    return jax.shard_map(
        body,
        mesh=mesh,
        in_specs=placed,
        out_specs=(
            P(every, None, None),
            P(shard, None),
            P(dp, shard),
            P(shard, dp),
            P(),
            P(),
            P(),
        ),
        check_vma=False,
    )
```

```python
import jax
import jax.numpy as jnp
from jax import lax
from jax.experimental import pallas as pl
from jax.experimental.pallas import tpu as pltpu
from jax.sharding import PartitionSpec as P

F = 128
K = 8
NF = 16
CAP = 32
LANES = 128


def layer_norm(flat):
    center = flat - jnp.mean(flat, axis=1, keepdims=True)
    inverse_std = lax.rsqrt(jnp.mean(center * center, axis=1, keepdims=True) + 1e-05)
    return (center * inverse_std, inverse_std)


def exchange(blocks, axis):
    return lax.all_to_all(blocks, axis, split_axis=0, concat_axis=0, tiled=True)


def spread(block, axis):
    count = lax.axis_size(axis)
    return exchange(jnp.broadcast_to(block[None], (count, *block.shape)), axis)


def gather(block, axis):
    return lax.all_gather(block, axis, axis=0, tiled=True)


def scatter(blocks, axis):
    return lax.psum_scatter(blocks, axis, scatter_dimension=0, tiled=True)


def halves(value):
    high = lax.reduce_precision(value, 8, 7)
    return jnp.concatenate([high, value - high], axis=-1).astype(jnp.bfloat16)


def halved(blocks, axis):
    count, place = lax.axis_size(axis), lax.axis_index(axis)
    step = count // 2
    while step:
        blocks = blocks.reshape(2, -1, blocks.shape[-1])
        side = place // step % 2
        keep = lax.dynamic_index_in_dim(blocks, side, keepdims=False)
        send = lax.dynamic_index_in_dim(blocks, 1 - side, keepdims=False)
        other = lax.ppermute(send, axis, [(i, i ^ step) for i in range(count)])
        blocks = (keep.astype(jnp.float32) + other.astype(jnp.float32)).astype(jnp.bfloat16)
        step //= 2
    return blocks


def network_kernel(ring, weights, lcb, back, mine):
    f32, bf16 = jnp.float32, jnp.bfloat16
    samples, columns = ring.shape
    split, taps = F * K, weights.shape[0]
    cross = (((1,), (1,)), ((), ()))
    preact = lax.dot_general(
        ring[:, :split], weights[:, :split], cross, preferred_element_type=f32
    )
    d_hidden = lax.dot_general(
        ring[:, split:], weights[:, split:], cross, preferred_element_type=f32
    )
    sigmoid = 1.0 / (1.0 + jnp.exp(-preact))
    activ = (preact * sigmoid).astype(bf16)
    d_pre = (d_hidden * sigmoid * (1.0 + preact * (1.0 - sigmoid))).astype(bf16)
    mine[:, :columns] = ring[...]
    mine[:, columns : columns + taps] = activ
    mine[:, columns + taps :] = d_pre
    back[:, :split] = jnp.dot(d_pre, weights[:, :split], preferred_element_type=f32).astype(bf16)
    for start in range(split, columns, 512):
        back[:, start : start + 512] = jnp.dot(
            activ, weights[:, start : start + 512], preferred_element_type=f32
        ).astype(bf16)
    back[:, columns:] = lcb[...]


def network(ring, weights, lcb):
    samples, columns = ring.shape
    taps = weights.shape[0]
    shape = lambda width: jax.ShapeDtypeStruct((samples, width), jnp.bfloat16)
    return pl.pallas_call(
        network_kernel,
        out_shape=(shape(columns + lcb.shape[1]), shape(columns + 2 * taps)),
        compiler_params=pltpu.CompilerParams(vmem_limit_bytes=32 * 2**20),
        cost_estimate=pl.CostEstimate(
            flops=4 * samples * taps * columns, bytes_accessed=7_000_000, transcendentals=65536
        ),
    )(ring, weights, lcb)


def weight_kernel(me, mine, other, activ, activ_other, d_pre, d_pre_other, out):
    depth = out.shape[0]
    f32 = jnp.float32
    along = (((0,), (0,)), ((), ()))
    first = me[0] == 0
    split, columns = F * K, mine.shape[1]
    start = 0
    for begin, end, right, right_other in (
        (split, columns, activ, activ_other),
        (0, split, d_pre, d_pre_other),
    ):
        rows = (end - begin) // (2 * depth)
        for z in range(depth):
            at = slice(begin + z * 2 * rows, begin + (z + 1) * 2 * rows)
            part = lax.dot_general(mine[:, at], right[...], along, preferred_element_type=f32)
            part = part + lax.dot_general(
                other[:, at], right_other[...], along, preferred_element_type=f32
            )
            part = jnp.where(first, part[:rows], part[rows:])
            out[z, 0, start : start + rows] = part.astype(jnp.bfloat16)
        start += rows


def weight_products(mine, other, hidden, far, depth):
    samples = mine.shape[0]
    columns = mine.shape[1] - 2 * far * hidden
    rows = columns // (2 * depth)
    first = columns // hidden
    ring = pl.BlockSpec((samples, columns), lambda j: (0, 0))
    activ = pl.BlockSpec((samples, hidden), lambda j: (0, first + j))
    d_pre = pl.BlockSpec((samples, hidden), lambda j: (0, first + far + j))
    return pl.pallas_call(
        weight_kernel,
        grid=(far,),
        in_specs=[
            pl.BlockSpec(memory_space=pltpu.SMEM), ring, ring, activ, activ, d_pre, d_pre
        ],
        out_specs=pl.BlockSpec((depth, 1, rows, hidden), lambda j: (0, j, 0, 0)),
        out_shape=jax.ShapeDtypeStruct((depth, far, rows, hidden), jnp.bfloat16),
        compiler_params=pltpu.CompilerParams(vmem_limit_bytes=32 * 2**20),
        cost_estimate=pl.CostEstimate(
            flops=8 * samples * rows * depth * far * hidden,
            bytes_accessed=6_000_000,
            transcendentals=0,
        ),
    )(lax.axis_index("core").reshape(1), mine, other, mine, other, mine, other)


def body(
    table, slot_rows, slot_counts, positions, fm_proj, ln_gain, w_up, w_down, w_lcb, cotangent
):
    highest = lax.Precision.HIGHEST
    f32, bf16 = jnp.float32, jnp.bfloat16
    shard, dp = ("x", "y"), ("z", "core")
    far, near = lax.axis_size("x"), lax.axis_size("y")
    depth = lax.axis_size("z")
    members, groups = far * near, depth * lax.axis_size("core")
    batch = positions.shape[0]
    width = table.shape[1]
    rows_here = table.shape[0]
    slots = members * CAP
    hidden = w_up.shape[1]
    request = slot_rows.reshape(members, CAP)
    counts_here = slot_counts.reshape(members)

    grad_mlp = cotangent[:, :NF, :].reshape(batch, NF * width)
    weights = gather(jnp.concatenate([w_up.T, w_down], axis=1), "x")

    asked = exchange(request, shard).reshape(slots)
    row_ids = lax.broadcasted_iota(jnp.int32, (slots, rows_here), 1)
    asked_hot = (asked[:, None] == row_ids).astype(bf16)
    sent = jnp.dot(asked_hot, table, preferred_element_type=f32).astype(bf16)
    fetched = exchange(sent.reshape(members, CAP, width), shard)
    live_mask = lax.broadcasted_iota(jnp.int32, (members, CAP), 1) < counts_here[:, None]
    fetched = jnp.where(live_mask[:, :, None], fetched, jnp.zeros((), bf16)).reshape(slots, width)
    flat_positions = positions.reshape(batch * F)
    slot_ids = lax.broadcasted_iota(jnp.int32, (batch * F, slots), 1)
    slot_hot = (flat_positions[:, None] == slot_ids).astype(bf16)
    embeds = jnp.dot(slot_hot, fetched, preferred_element_type=f32).astype(bf16)
    embeds = embeds.reshape(batch, F, width)

    embeds_f = embeds.astype(f32)
    projector = fm_proj.astype(f32)
    compressed = jnp.einsum("bfd,fk->bdk", embeds, fm_proj, preferred_element_type=f32)
    gram = jnp.einsum("bfd,bdk->bfk", embeds_f, compressed, precision=highest).reshape(batch, F * K)
    normal_part, inverse_std = layer_norm(gram)
    normed = (normal_part * ln_gain).astype(bf16)
    ring = spread(jnp.concatenate([normed, grad_mlp], axis=1), "y")
    ring = ring.reshape(near * batch, -1)

    grad_linear = cotangent[:, NF:, :]
    linear_part = jnp.einsum("lf,bfd->bld", w_lcb, embeds, preferred_element_type=f32)
    lcb_part = jnp.einsum("bld,bfd->lf", grad_linear, embeds, preferred_element_type=f32)
    lcb_part = lcb_part.astype(bf16).reshape(near * batch, -1)
    spare = -lcb_part.shape[1] % LANES
    lcb_padded = jnp.pad(lcb_part, ((0, 0), (0, spare)))
    back, mine = network(ring, weights, lcb_padded)
    back = exchange(back.reshape(near, batch, -1), "y")
    other = lax.ppermute(mine, "core", [(0, 1), (1, 0)])
    weight_sum = weight_products(mine, other, hidden, far, depth).reshape(-1, hidden)
    back, _ = lax.optimization_barrier((back, weight_sum))
    weight_sum = scatter(weight_sum, "z")
    back = jnp.sum(back.astype(f32), axis=0)
    split, end = F * K, F * K + NF * width
    d_normed, mlp_out = back[:, :split], back[:, split:end]
    lcb_mine = back[:, end : end + lcb_part.shape[1]].astype(bf16)
    d_linear = jnp.einsum("lf,bld->bfd", w_lcb, grad_linear, preferred_element_type=f32)

    gain_part = jnp.sum(d_normed * normal_part, axis=0)
    scaled = d_normed * ln_gain
    d_gram = inverse_std * (
        scaled
        - jnp.mean(scaled, axis=1, keepdims=True)
        - normal_part * jnp.mean(scaled * normal_part, axis=1, keepdims=True)
    )
    d_gram = d_gram.reshape(batch, F, K)
    d_compressed = jnp.einsum("bfd,bfk->bdk", embeds_f, d_gram, precision=highest)
    d_embeds = cotangent.astype(f32) + d_linear
    d_embeds = d_embeds + jnp.einsum("bfk,bdk->bfd", d_gram, compressed, precision=highest)
    d_embeds = d_embeds + jnp.einsum("fk,bdk->bfd", projector, d_compressed, precision=highest)
    d_embeds = d_embeds.astype(bf16).reshape(batch * F, width)
    slot_rows_hot = (
        lax.broadcasted_iota(jnp.int32, (slots, batch * F), 0) == flat_positions[None, :]
    ).astype(bf16)
    slot_grad = jnp.dot(slot_rows_hot, d_embeds, preferred_element_type=f32)
    slot_grad = slot_grad.reshape(members, CAP, width)
    slot_grad = jnp.where(live_mask[:, :, None], slot_grad, 0.0).astype(bf16)
    proj_part = jnp.einsum("bfd,bdk->fk", embeds, halves(d_compressed), preferred_element_type=f32)
    proj_part = proj_part[:, :K] + proj_part[:, K:]
    small = jnp.concatenate([gain_part, proj_part.reshape(-1)]).astype(bf16).reshape(CAP, -1)
    row = 2 * LANES
    lcb_mine = lcb_mine.reshape(-1, row)
    lcb_mine = jnp.pad(lcb_mine, ((0, -lcb_mine.shape[0] % 8), (0, 0)))
    small = jnp.pad(small, ((0, 0), (0, row - width - small.shape[1])))
    sent = jnp.concatenate([slot_grad, jnp.broadcast_to(small[None], (members, *small.shape))], axis=2)
    lcb_sent = jnp.broadcast_to(lcb_mine[None], (members, *lcb_mine.shape))
    received = exchange(jnp.concatenate([sent, lcb_sent], axis=1), shard)
    returned = received[:, :CAP, :width].reshape(slots, width)
    small_end = width + 2 * F * K // CAP
    small = jnp.sum(received[:, :CAP, width:small_end].astype(f32), axis=0).astype(bf16)
    lcb = received[:, CAP:].reshape(far, near, -1)[:, :, : (F - NF) * F // near]
    lcb = jnp.sum(lcb.astype(f32), axis=0).astype(bf16)
    small = jnp.concatenate([small.reshape(-1), lcb.reshape(-1)]).reshape(groups, -1, LANES)
    row_hot = (
        lax.broadcasted_iota(jnp.int32, (rows_here, slots), 0) == asked[None, :]
    ).astype(bf16)
    table_part = lax.dot_general(
        returned, row_hot, (((0,), (1,)), ((), ())), preferred_element_type=f32
    ).astype(bf16)
    columns = rows_here // LANES
    table_part = table_part.reshape(width, columns, LANES).transpose(1, 0, 2)
    table_part = table_part.reshape(groups, -1, LANES)
    held = table_part.shape[1]
    total = jnp.concatenate([table_part, small], axis=1)
    total, weight_sum = lax.optimization_barrier((total, weight_sum))
    weight_sum = halved(weight_sum, "x")
    total = exchange(total, dp)
    total = jnp.sum(total.astype(f32), axis=0).astype(bf16)
    total, weight_sum = lax.optimization_barrier((total, weight_sum))
    total = spread(total, dp)
    down_count = NF * width // groups
    grad_w_down = weight_sum[:down_count].T
    grad_w_up = weight_sum[down_count:]
    table_all = total[:, :held].reshape(columns, width, LANES)
    grad_table = table_all.transpose(0, 2, 1).reshape(rows_here, width).astype(f32)
    small = total[:, held:].reshape(-1).astype(f32)
    grad_ln_gain = small[: F * K]
    grad_fm_proj = small[F * K : 2 * F * K].reshape(F, K)
    grad_w_lcb = small[2 * F * K :].reshape(F - NF, F)

    joined = jnp.concatenate([mlp_out.reshape(batch, NF, width), linear_part], axis=1)
    mixed = (embeds_f + joined).astype(bf16)
    return (mixed, grad_table, grad_w_up, grad_w_down, grad_fm_proj, grad_w_lcb, grad_ln_gain)


def solution(mesh):
    dp, shard = mesh.devices.shape
    near = min(8, shard // 2)
    split = (dp // 2, 2, shard // near, near)
    dp, shard = ("z", "core"), ("x", "y")
    mesh = jax.sharding.Mesh(mesh.devices.reshape(split), (*dp, *shard))
    every = (*dp, *shard)
    placed = (
        P(shard, None),
        P(dp, shard, None, None),
        P(dp, shard, None),
        P(every, None),
        P(),
        P(),
        P(None, shard),
        P(shard, None),
        P(),
        P(every, None, None),
    )
    return jax.shard_map(
        body,
        mesh=mesh,
        in_specs=placed,
        out_specs=(
            P(every, None, None),
            P(shard, None),
            P(dp, shard),
            P(shard, dp),
            P(),
            P(),
            P(),
        ),
        check_vma=False,
    )
```
